32 devices in a mesh: groups: 2 (over y), expert: 8 (over z, x), dp: 2 (over core).
Axes of the slice: x: 2, y: 2, z: 4, core: 2. Of those that a mesh axis runs over, the one named last changes fastest.
Arguments:
- tokens: bfloat16 [4096, 2880], P(('groups', 'expert', 'dp')), parts along dimension 0, may hold values from -6 to 6
- cotangent: bfloat16 [4096, 2880], P(('groups', 'expert', 'dp')), parts along dimension 0, may hold values from -1.5 to 1.5
- expert_ids: int32 [4096, 4], P(('groups', 'expert', 'dp')), parts along dimension 0, may hold values from 0 to 127, as said below
- route_weight: float32 [4096, 4], P(('groups', 'expert', 'dp')), parts along dimension 0, may hold values from 0.1 to 1
- gate_weight: bfloat16 [20480, 2880], P(('expert', 'dp')), may hold values from -0.109375 to 0.109375
- up_weight: bfloat16 [20480, 2880], P(('expert', 'dp')), may hold values from -0.109375 to 0.109375
- down_weight: bfloat16 [20480, 2880], P(('expert', 'dp')), may hold values from -0.125 to 0.125
Outputs:
- grad_tokens: bfloat16 [4096, 2880], P(('groups', 'expert', 'dp')), parts along dimension 0
- grad_gate: bfloat16 [40960, 2880], P(('groups', 'expert', 'dp')), parts along dimension 0
- grad_up: bfloat16 [40960, 2880], P(('groups', 'expert', 'dp')), parts along dimension 0
- grad_down: bfloat16 [40960, 2880], P(('groups', 'expert', 'dp')), parts along dimension 0
The draws below stay inside these ranges and needn't reach their ends.
There are 2 independent parts, one for each index of `groups`. The reference program is written for one: setup_inputs(seed, part) draws one part's arguments, and reference() takes and returns one part's arrays. A program takes and returns all parts, laid end to end along the dimension named above; an argument that names none is the same for every part. Nothing has to cross between parts.
Inputs may be any that keep to these rules, and one draw needn't show every extreme that they name: `expert_ids`: the 4 ids of a token are distinct and differ modulo 4. In each aligned block of 128 tokens (the tokens of one device) each expert below 8 is named at least once and at most 4 times; one of them, the same in every block, is named exactly 4 times in every block.
All inputs are finite; a program needn't handle non-finite values.
Results may differ from the reference program's by a relative error of at most 0.0066.
Values may be sent and summed in bfloat16 or wider, within the bound.
A program may use at most 256 MiB of HBM per device.

```python
import jax
import jax.numpy as jnp
from jax import lax

D = 2880
FF = 2560
EXPERTS_ALL = 128
E_WIN = 8
TOP = 4
TOK_DEV = 128
CAP = 4
TOKENS = 2048
N_EXPERT = 8
N_DP = 2


def draw_expert_ids(key, part):
    key = jax.random.fold_in(key, 11)
    key_hot, key_count, key_order, key_other, key_shuffle = jax.random.split(key, 5)
    blocks = TOKENS // TOK_DEV
    spread = max(CAP // 2, 1)
    hottest = jax.random.randint(key_hot, (), 0, E_WIN)
    counts = 1 + jax.random.randint(key_count, (blocks, E_WIN), 0, spread)
    counts = jnp.where(jnp.arange(E_WIN, dtype=jnp.int32)[None, :] == hottest, CAP, counts)
    scores = jax.random.randint(key_order, (blocks, TOP, TOK_DEV), 0, 1 << 16) * TOK_DEV + jnp.arange(TOK_DEV, dtype=jnp.int32)[None, None, :]
    position = jnp.argsort(jnp.argsort(scores, axis=-1), axis=-1)
    first = counts[:, :TOP][:, :, None]
    second = counts[:, TOP:][:, :, None]
    column = jnp.arange(TOP, dtype=jnp.int32)[None, :, None]
    outside = E_WIN + TOP * jax.random.randint(key_other, (blocks, TOP, TOK_DEV), 0, (EXPERTS_ALL - E_WIN) // TOP) + column
    chosen = jnp.where(position < first, column, jnp.where(position < first + second, column + TOP, outside))
    chosen = jnp.transpose(chosen, (0, 2, 1)).reshape(TOKENS, TOP)
    shuffle = jax.random.randint(key_shuffle, (TOKENS, TOP), 0, 1 << 16) * TOP + jnp.arange(TOP, dtype=jnp.int32)[None, :]
    order = jnp.argsort(shuffle, axis=-1)
    return jnp.take_along_axis(chosen, order, axis=-1).astype(jnp.int32)


def block_levels(stream_key, dims, cuts, smallest, top_value):
    gain, own = 1.0, jax.random.fold_in(stream_key, 6)
    for dim, blocks in cuts:
        heights = jnp.exp(jax.random.uniform(jax.random.fold_in(own, dim), (blocks,), jnp.float32, smallest / len(cuts), top_value / len(cuts)))
        gain = gain * jnp.repeat(heights, dims[dim] // blocks).reshape([-1 if axis == dim else 1 for axis in range(len(dims))])
    return gain


def scatter_about(own_key, shape, width, most, pieces=(), kind=jnp.bfloat16):
    result = jax.random.normal(own_key, shape, jnp.float32) * width
    if len(pieces) > 0:
        result = block_levels(own_key, shape, pieces, -0.22, 0.18) * result
    return jnp.clip(result, min=-most, max=most).astype(kind)


def setup_inputs(seed: int = 0, part: int = 0) -> dict:
    streams_of = jax.random.split(jax.random.key(seed), 8)
    part_keys = jax.random.split(jax.random.fold_in(streams_of[7], part), 8)
    return {
        "tokens": scatter_about(part_keys[0], (TOKENS, D), 1.0, 6.0, ((0, 16),)),
        "cotangent": scatter_about(part_keys[1], (TOKENS, D), 0.25, 1.5, ((0, 16),)),
        "expert_ids": draw_expert_ids(jax.random.fold_in(jax.random.fold_in(streams_of[7], part), 71), part),
        "route_weight": jnp.clip(0.1 + 0.9 * jax.random.uniform(part_keys[3], (TOKENS, TOP), jnp.float32) ** block_levels(part_keys[3], (TOKENS, TOP), ((0, 16),), -0.2, 0.2), 0.1, 1.0),
        "gate_weight": scatter_about(streams_of[4], (E_WIN * FF, D), D ** -0.5, 0.109375, ((0, 16),)),
        "up_weight": scatter_about(streams_of[5], (E_WIN * FF, D), D ** -0.5, 0.109375, ((0, 16),)),
        "down_weight": scatter_about(streams_of[6], (E_WIN * FF, D), FF ** -0.5, 0.125, ((0, 16),)),
    }


def expert_rows(tokens, cotangent, expert_ids, route_weight, owner, expert_index, slots):
    matches = expert_ids[owner] == expert_index
    member = jnp.any(matches, axis=1)
    weight_of = jnp.sum(jnp.where(matches, route_weight[owner], 0.0), axis=1)
    picked = jnp.nonzero(member, size=slots, fill_value=0)[0].astype(jnp.int32)
    valid = (jnp.arange(slots, dtype=jnp.int32) < jnp.sum(member.astype(jnp.int32)))[:, None]
    global_rows = owner[picked]
    rows_x = jnp.where(valid, tokens[global_rows], jnp.zeros((), jnp.bfloat16))
    scaled = jnp.where(valid, weight_of[picked][:, None] * cotangent[global_rows].astype(jnp.float32), 0.0).astype(jnp.bfloat16)
    return global_rows, rows_x, scaled


def reference(tokens, cotangent, expert_ids, route_weight, gate_weight, up_weight, down_weight):
    group_size = N_EXPERT // E_WIN
    hidden_block = FF // group_size
    rounds = TOKENS // (TOK_DEV * N_DP)
    slots = rounds * CAP
    local_rows = jnp.arange(rounds * TOK_DEV, dtype=jnp.int32)
    contract_last = (((1,), (1,)), ((), ()))
    contract_first = (((0,), (0,)), ((), ()))

    def expert_step(carry, expert_index):
        w_gate = lax.dynamic_slice_in_dim(gate_weight, expert_index * FF, FF, 0)
        w_up = lax.dynamic_slice_in_dim(up_weight, expert_index * FF, FF, 0)
        w_down = lax.dynamic_slice_in_dim(down_weight, expert_index * FF, FF, 0)
        share_gate = jnp.zeros((FF, D), jnp.float32)
        share_up = jnp.zeros((FF, D), jnp.float32)
        share_down = jnp.zeros((FF, D), jnp.float32)
        for replica in range(N_DP):
            owner = (local_rows // TOK_DEV * N_DP + replica) * TOK_DEV + local_rows % TOK_DEV
            global_rows, rows_x, scaled = expert_rows(tokens, cotangent, expert_ids, route_weight, owner, expert_index, slots)
            gate_pre = lax.dot_general(rows_x, w_gate, contract_last, preferred_element_type=jnp.float32)
            up_pre = lax.dot_general(rows_x, w_up, contract_last, preferred_element_type=jnp.float32)
            d_act = lax.dot_general(scaled, w_down, contract_last, preferred_element_type=jnp.float32)
            sigmoid_gate = jax.nn.sigmoid(1.702 * gate_pre)
            gated = gate_pre * sigmoid_gate
            activation = ((up_pre + 1.0) * gated).astype(jnp.bfloat16)
            d_up = (d_act * gated).astype(jnp.bfloat16)
            d_gate = (d_act * (up_pre + 1.0) * (sigmoid_gate + 1.702 * gate_pre * sigmoid_gate * (1.0 - sigmoid_gate))).astype(jnp.bfloat16)
            blocks_gate = d_gate.astype(jnp.float32).reshape(slots, group_size, hidden_block)
            blocks_up = d_up.astype(jnp.float32).reshape(slots, group_size, hidden_block)
            parts = jnp.einsum("rsh,shd->rsd", blocks_gate, w_gate.astype(jnp.float32).reshape(group_size, hidden_block, D))
            parts = parts + jnp.einsum("rsh,shd->rsd", blocks_up, w_up.astype(jnp.float32).reshape(group_size, hidden_block, D))
            rounded = lax.optimization_barrier(parts.astype(jnp.bfloat16))
            carry = carry.at[global_rows].add(jnp.sum(rounded.astype(jnp.float32), axis=1))
            term_gate = lax.dot_general(d_gate, rows_x, contract_first, preferred_element_type=jnp.float32).astype(jnp.bfloat16)
            term_up = lax.dot_general(d_up, rows_x, contract_first, preferred_element_type=jnp.float32).astype(jnp.bfloat16)
            term_down = lax.dot_general(activation, scaled, contract_first, preferred_element_type=jnp.float32).astype(jnp.bfloat16)
            share_gate = share_gate + lax.optimization_barrier(term_gate).astype(jnp.float32)
            share_up = share_up + lax.optimization_barrier(term_up).astype(jnp.float32)
            share_down = share_down + lax.optimization_barrier(term_down).astype(jnp.float32)
        return carry, (share_gate.astype(jnp.bfloat16), share_up.astype(jnp.bfloat16), share_down.astype(jnp.bfloat16))

    total, shares = lax.scan(expert_step, jnp.zeros((TOKENS, D), jnp.float32), jnp.arange(E_WIN, dtype=jnp.int32))
    grad_gate = shares[0].reshape(E_WIN * FF, D)
    grad_up = shares[1].reshape(E_WIN * FF, D)
    grad_down = shares[2].reshape(E_WIN * FF, D)
    return (total.astype(jnp.bfloat16), grad_gate, grad_up, grad_down)
```

```python
import functools

import jax
import jax.numpy as jnp
from jax import lax
from jax.experimental import pallas as pl
from jax.experimental.pallas import tpu as pltpu
from jax.sharding import PartitionSpec as P

E_WIN = 8
CAP = 4
FOLD = 4
BLOCK = FOLD * CAP
LAST = (((1,), (1,)), ((), ()))
FIRST = (((0,), (0,)), ((), ()))
F32 = jnp.float32
BF16 = jnp.bfloat16


def fold_columns(width):
    step = -(-width // (FOLD * 128)) * 128
    return [(j * step, min(width, (j + 1) * step)) for j in range(FOLD)]


def iota(shape, dim):
    return lax.broadcasted_iota(jnp.int32, shape, dim)


def dot(a, b):
    return jnp.dot(a, b, preferred_element_type=F32)


def exchange_kernel(
    experts, chunk,
    tok, cot, ids, route, gate_hbm, up_hbm, down_hbm,
    grad_tok, d_gate_out, d_up_out, act_out, x_out, c_out,
    gate_w, up_w, down_w, send_x, send_c, recv_x, recv_c, stage,
    gate_pre, up_pre, total, half_out, half_in, ret_out, ret_in,
    w_sem, xs_sem, xr_sem, cs_sem, cr_sem, xfs_sem, xfr_sem, cfs_sem, cfr_sem,
    half_sem, rs_sem, rr_sem,
):
    me = lax.axis_index("expert")
    core = lax.axis_index("dp")
    peer = 1 - core
    n_tok, width = tok.shape
    units = gate_hbm.shape[0]
    chunks = units // chunk
    cols = fold_columns(width)
    lines = experts * BLOCK
    own_rows = experts * CAP
    peer_id = {"dp": peer}

    barrier = pltpu.get_barrier_semaphore()
    for d in range(1, experts):
        pl.semaphore_signal(
            barrier, inc=1, device_id={"expert": lax.rem(me + d, experts)},
            device_id_type=pl.DeviceIdType.MESH,
        )
    pl.semaphore_signal(barrier, inc=1, device_id=peer_id, device_id_type=pl.DeviceIdType.MESH)

    def weight_copy(which, c):
        src = (gate_hbm, up_hbm, down_hbm)[which]
        dst = (gate_w, up_w, down_w)[which]
        rows = pl.ds(pl.multiple_of(c * chunk, chunk), chunk)
        return pltpu.make_async_copy(src.at[rows], dst.at[rows], w_sem.at[which, c])

    for which in range(3):
        for c in range(chunks):
            weight_copy(which, c).start()

    line = iota((n_tok, lines), 1)
    line_expert = line // BLOCK
    line_slot = (line % CAP).astype(F32)
    line_fold = (line // CAP) % FOLD
    member = jnp.zeros((n_tok, lines), F32)
    weight = jnp.zeros((n_tok, lines), F32)
    for p in range(ids.shape[1]):
        hit = ids[:, p : p + 1] == line_expert
        member += jnp.where(hit, 1.0, 0.0)
        weight += jnp.where(hit, route[:, p : p + 1], 0.0)
    earlier = jnp.where(iota((n_tok, n_tok), 0) > iota((n_tok, n_tok), 1), 1.0, 0.0)
    position = dot(earlier.astype(BF16), member.astype(BF16))
    place_t = jnp.where(position == line_slot, member, 0.0)
    place = place_t.T
    slot_weight = jnp.sum((place_t * weight).T, axis=1, keepdims=True)
    fold_of = (iota((lines, n_tok), 0) // CAP) % FOLD
    picks = [jnp.where(fold_of == j, place, 0.0).astype(BF16) for j in range(FOLD)]

    def pack(selects, source):
        full = dot(selects[0], source[:, cols[0][0] : cols[0][1]])
        for j in range(1, FOLD - 1):
            full += dot(selects[j], source[:, cols[j][0] : cols[j][1]])
        stage[...] = full
        lo, hi = cols[FOLD - 1]
        stage[:, : hi - lo] += dot(selects[FOLD - 1], source[:, lo:hi])
        return stage[...]

    def block(index):
        return pl.ds(pl.multiple_of(index * BLOCK, BLOCK), BLOCK)

    def slot(src):
        return block(core * experts + src)

    def row_send(send, recv, s_sem, r_sem, d):
        to = lax.rem(me + d, experts)
        return pltpu.make_async_remote_copy(
            src_ref=send.at[block(to)], dst_ref=recv.at[slot(me)],
            send_sem=s_sem.at[d], recv_sem=r_sem.at[d],
            device_id={"expert": to}, device_id_type=pl.DeviceIdType.MESH,
        )

    def row_arrival(send, recv, s_sem, r_sem, d):
        origin = lax.rem(me + experts - d, experts)
        return pltpu.make_async_remote_copy(
            src_ref=send.at[block(origin)], dst_ref=recv.at[slot(origin)],
            send_sem=s_sem.at[d], recv_sem=r_sem.at[d],
            device_id={"expert": origin}, device_id_type=pl.DeviceIdType.MESH,
        )

    def forward(recv, s_sem, r_sem, d):
        origin = lax.rem(me + experts - d, experts)
        return pltpu.make_async_remote_copy(
            src_ref=recv.at[slot(origin)], dst_ref=recv.at[slot(origin)],
            send_sem=s_sem.at[d], recv_sem=r_sem.at[d],
            device_id=peer_id, device_id_type=pl.DeviceIdType.MESH,
        )

    def forward_arrival(recv, s_sem, r_sem, d):
        origin = lax.rem(me + experts - d, experts)
        where = block(peer * experts + origin)
        return pltpu.make_async_remote_copy(
            src_ref=recv.at[where], dst_ref=recv.at[where],
            send_sem=s_sem.at[d], recv_sem=r_sem.at[d],
            device_id=peer_id, device_id_type=pl.DeviceIdType.MESH,
        )

    x_sems = (xs_sem, xr_sem)
    c_sems = (cs_sem, cr_sem)
    xf_sems = (xfs_sem, xfr_sem)
    cf_sems = (cfs_sem, cfr_sem)
    near_last = sorted(range(1, experts), key=lambda d: abs(2 * d - experts))

    send_x[...] = pack(picks, tok).astype(BF16)
    recv_x[slot(me), :] = send_x[block(me), :]
    pl.semaphore_wait(barrier, experts)
    for d in near_last:
        row_send(send_x, recv_x, *x_sems, d).start()
    forward(recv_x, *xf_sems, 0).start()
    send_c[...] = (pack(picks, cot) * slot_weight).astype(BF16)
    recv_c[slot(me), :] = send_c[block(me), :]
    for d in near_last:
        row_send(send_c, recv_c, *c_sems, d).start()
    forward(recv_c, *cf_sems, 0).start()

    all_rows = 2 * own_rows
    row = iota((all_rows, 2 * lines), 0)
    line_of = iota((all_rows, 2 * lines), 1)
    base = (row // CAP) * BLOCK + row % CAP

    def unpack(recv, out):
        for j, (lo, hi) in enumerate(cols):
            select = jnp.where(line_of == base + j * CAP, 1.0, 0.0).astype(BF16)
            out[:, lo:hi] = dot(select, recv[:, : hi - lo]).astype(BF16)

    def gather(send, recv, sems, f_sems, out):
        for d in near_last[::-1]:
            row_arrival(send, recv, *sems, d).wait_recv()
            forward(recv, *f_sems, d).start()
        for d in range(experts):
            forward_arrival(recv, *f_sems, d).wait_recv()
        unpack(recv, out)

    gather(send_x, recv_x, x_sems, xf_sems, x_out)

    def span(c):
        return pl.ds(pl.multiple_of(c * chunk, chunk), chunk)

    def project(c, carry):
        weight_copy(0, c).wait()
        weight_copy(1, c).wait()
        x = x_out[...]
        gate_pre[:, span(c)] = lax.dot_general(x, gate_w[span(c), :], LAST, preferred_element_type=F32)
        up_pre[:, span(c)] = lax.dot_general(x, up_w[span(c), :], LAST, preferred_element_type=F32)
        return carry

    lax.fori_loop(0, chunks, project, 0)
    gather(send_c, recv_c, c_sems, cf_sems, c_out)

    total[...] = jnp.zeros_like(total)

    def backward(c, carry):
        weight_copy(2, c).wait()
        d_act = lax.dot_general(
            c_out[...], down_w[span(c), :], LAST, preferred_element_type=F32
        )
        gate = gate_pre[:, span(c)]
        up = up_pre[:, span(c)] + 1.0
        sig = jax.nn.sigmoid(1.702 * gate)
        gated = gate * sig
        act_out[:, span(c)] = (up * gated).astype(BF16)
        d_up = (d_act * gated).astype(BF16)
        d_gate = (d_act * up * (sig + 1.702 * gate * sig * (1.0 - sig))).astype(BF16)
        d_up_out[:, span(c)] = d_up
        d_gate_out[:, span(c)] = d_gate
        total[...] += dot(d_gate, gate_w[span(c), :]) + dot(d_up, up_w[span(c), :])
        return carry

    lax.fori_loop(0, chunks, backward, 0)

    def half_rows(which):
        return pl.ds(pl.multiple_of(which * own_rows, own_rows), own_rows)

    half_out[...] = total[half_rows(peer), :].astype(BF16)
    swap = pltpu.make_async_remote_copy(
        src_ref=half_out, dst_ref=half_in, send_sem=half_sem.at[0], recv_sem=half_sem.at[1],
        device_id=peer_id, device_id_type=pl.DeviceIdType.MESH,
    )
    swap.start()
    swap.wait()
    half_out[...] = (total[half_rows(core), :] + half_in[...].astype(F32)).astype(BF16)

    out_line = iota((lines, own_rows), 0)
    wanted = (out_line // BLOCK) * CAP + out_line % CAP
    matched = wanted == iota((lines, own_rows), 1)
    out_fold = (out_line // CAP) % FOLD
    puts = [
        jnp.where(jnp.logical_and(matched, out_fold == j), 1.0, 0.0).astype(BF16)
        for j in range(FOLD)
    ]
    ret_out[...] = pack(puts, half_out).astype(BF16)
    ret_in[block(me), :] = ret_out[block(me), :]

    def ret_copy(d, sending):
        other = lax.rem(me + d, experts) if sending else lax.rem(me + experts - d, experts)
        return pltpu.make_async_remote_copy(
            src_ref=ret_out.at[block(other)], dst_ref=ret_in.at[block(me if sending else other)],
            send_sem=rs_sem.at[d], recv_sem=rr_sem.at[d],
            device_id={"expert": other}, device_id_type=pl.DeviceIdType.MESH,
        )

    for d in near_last:
        ret_copy(d, True).start()
    for d in range(1, experts):
        row_send(send_x, recv_x, *x_sems, d).wait_send()
        row_send(send_c, recv_c, *c_sems, d).wait_send()
    for d in range(experts):
        forward(recv_x, *xf_sems, d).wait_send()
        forward(recv_c, *cf_sems, d).wait_send()
    for d in range(1, experts):
        ret_copy(d, False).wait_recv()
    for j, (lo, hi) in enumerate(cols):
        take = jnp.where(line_fold == j, place_t, 0.0).astype(BF16)
        grad_tok[:, lo:hi] = dot(take, ret_in[:, : hi - lo]).astype(BF16)
    for d in range(1, experts):
        ret_copy(d, True).wait_send()


def weight_kernel(d_gate, d_up, act, x, c, g_gate, g_up, g_down):
    def term(a, b):
        return lax.dot_general(a[...], b[...], FIRST, preferred_element_type=F32).astype(BF16)

    g_gate[...] = term(d_gate, x)
    g_up[...] = term(d_up, x)
    g_down[...] = term(act, c)


def kernel_body(tokens, cotangent, expert_ids, route_weight, gate_weight, up_weight, down_weight):
    experts = lax.axis_size("expert")
    n_tok, width = tokens.shape
    units = gate_weight.shape[0]
    chunk = 256
    rows = 2 * experts * CAP
    lines = experts * BLOCK
    lo, hi = fold_columns(width)[0]
    fold_width = hi - lo
    vmem = pl.BlockSpec(memory_space=pltpu.VMEM)
    hbm = pl.BlockSpec(memory_space=pl.ANY)
    sem = pltpu.SemaphoreType.DMA
    shape = jax.ShapeDtypeStruct
    grad_tokens, d_gate, d_up, act, x, c = pl.pallas_call(
        functools.partial(exchange_kernel, experts, chunk),
        out_shape=(
            shape((n_tok, width), BF16),
            shape((rows, units), BF16),
            shape((rows, units), BF16),
            shape((rows, units), BF16),
            shape((rows, width), BF16),
            shape((rows, width), BF16),
        ),
        in_specs=[vmem] * 4 + [hbm] * 3,
        out_specs=(vmem,) * 6,
        scratch_shapes=[
            pltpu.VMEM((units, width), BF16),
            pltpu.VMEM((units, width), BF16),
            pltpu.VMEM((units, width), BF16),
            pltpu.VMEM((lines, fold_width), BF16),
            pltpu.VMEM((lines, fold_width), BF16),
            pltpu.VMEM((2 * lines, fold_width), BF16),
            pltpu.VMEM((2 * lines, fold_width), BF16),
            pltpu.VMEM((lines, fold_width), F32),
            pltpu.VMEM((rows, units), F32),
            pltpu.VMEM((rows, units), F32),
            pltpu.VMEM((rows, width), F32),
            pltpu.VMEM((rows // 2, width), BF16),
            pltpu.VMEM((rows // 2, width), BF16),
            pltpu.VMEM((lines, fold_width), BF16),
            pltpu.VMEM((lines, fold_width), BF16),
            sem((3, units // chunk)),
            sem((experts,)), sem((experts,)), sem((experts,)), sem((experts,)),
            sem((experts,)), sem((experts,)), sem((experts,)), sem((experts,)),
            sem((2,)), sem((experts,)), sem((experts,)),
        ],
        compiler_params=pltpu.CompilerParams(
            collective_id=0, has_side_effects=True, vmem_limit_bytes=56 * 1024 * 1024
        ),
        name="exchange",
    )(tokens, cotangent, expert_ids, route_weight, gate_weight, up_weight, down_weight)

    step = 128
    part = pl.BlockSpec((rows, step), lambda i: (0, i))
    whole = pl.BlockSpec((rows, width), lambda i: (0, 0))
    result = pl.BlockSpec((step, width), lambda i: (i, 0))
    grads = pl.pallas_call(
        weight_kernel,
        out_shape=(shape((units, width), BF16),) * 3,
        grid=(units // step,),
        in_specs=[part, part, part, whole, whole],
        out_specs=(result,) * 3,
        compiler_params=pltpu.CompilerParams(vmem_limit_bytes=32 * 1024 * 1024),
        cost_estimate=pl.CostEstimate(
            flops=6 * rows * units * width, bytes_accessed=6 * units * width, transcendentals=0
        ),
        name="weight_grads",
    )(d_gate, d_up, act, x, c)
    return (grad_tokens, *grads)


def expert_backward(rows_x, rows_c, w_gate, w_up, w_down):
    contract_last = (((1,), (1,)), ((), ()))
    gate_pre = lax.dot_general(rows_x, w_gate, contract_last, preferred_element_type=jnp.float32)
    up_pre = lax.dot_general(rows_x, w_up, contract_last, preferred_element_type=jnp.float32)
    d_act = lax.dot_general(rows_c, w_down, contract_last, preferred_element_type=jnp.float32)
    sigmoid_gate = jax.nn.sigmoid(1.702 * gate_pre)
    gated = gate_pre * sigmoid_gate
    activation = ((up_pre + 1.0) * gated).astype(jnp.bfloat16)
    d_up = (d_act * gated).astype(jnp.bfloat16)
    d_gate = (
        d_act
        * (up_pre + 1.0)
        * (sigmoid_gate + 1.702 * gate_pre * sigmoid_gate * (1.0 - sigmoid_gate))
    ).astype(jnp.bfloat16)
    partial_value = jnp.dot(d_gate, w_gate, preferred_element_type=jnp.float32) + jnp.dot(
        d_up, w_up, preferred_element_type=jnp.float32
    )
    return (activation, d_gate, d_up, partial_value)


def weight_terms(rows_x, rows_c, activation, d_gate, d_up):
    contract_first = (((0,), (0,)), ((), ()))
    term_gate = lax.dot_general(
        d_gate, rows_x, contract_first, preferred_element_type=jnp.float32
    ).astype(jnp.bfloat16)
    term_up = lax.dot_general(
        d_up, rows_x, contract_first, preferred_element_type=jnp.float32
    ).astype(jnp.bfloat16)
    term_down = lax.dot_general(
        activation, rows_c, contract_first, preferred_element_type=jnp.float32
    ).astype(jnp.bfloat16)
    return lax.optimization_barrier((term_gate, term_up, term_down))


def body(tokens, cotangent, expert_ids, route_weight, gate_weight, up_weight, down_weight):
    devices = lax.axis_size("expert")
    group_size = devices // E_WIN
    model_width = tokens.shape[1]
    window_ids = jnp.arange(E_WIN, dtype=jnp.int32)
    matches = expert_ids[:, :, None] == window_ids[None, None, :]
    member = jnp.any(matches, axis=1)
    weight_of = jnp.sum(jnp.where(matches, route_weight[:, :, None], 0.0), axis=1)
    position = jnp.cumsum(member.astype(jnp.int32), axis=0) - 1
    slot_ids = jnp.arange(CAP, dtype=jnp.int32)
    placement = jnp.logical_and(
        member.T[:, None, :], position.T[:, None, :] == slot_ids[None, :, None]
    )
    place_half = placement.astype(jnp.bfloat16)
    place_full = placement.astype(jnp.float32)
    picked_x = jnp.einsum(
        "kct,td->kcd", place_half, tokens, preferred_element_type=jnp.float32
    ).astype(jnp.bfloat16)
    picked_dy = jnp.einsum("kct,td->kcd", place_half, cotangent, preferred_element_type=jnp.float32)
    slot_weight = jnp.einsum("kct,tk->kc", place_full, weight_of, precision=lax.Precision.HIGHEST)
    picked_c = (slot_weight[:, :, None] * picked_dy).astype(jnp.bfloat16)
    send_x = jnp.repeat(picked_x, group_size, axis=0)
    send_c = jnp.repeat(picked_c, group_size, axis=0)
    recv_x, recv_c = (
        lax.all_to_all(send_x, "expert", split_axis=0, concat_axis=0, tiled=True),
        lax.all_to_all(send_c, "expert", split_axis=0, concat_axis=0, tiled=True),
    )
    rows_x = recv_x.reshape(devices * CAP, model_width)
    rows_c = recv_c.reshape(devices * CAP, model_width)
    full_gate, full_up, full_down = (
        lax.all_gather(gate_weight, "dp", axis=0, tiled=True),
        lax.all_gather(up_weight, "dp", axis=0, tiled=True),
        lax.all_gather(down_weight, "dp", axis=0, tiled=True),
    )
    activation, d_gate, d_up, partial_value = expert_backward(
        rows_x, rows_c, full_gate, full_up, full_down
    )
    part_rows = partial_value.astype(jnp.bfloat16)
    term_gate, term_up, term_down = weight_terms(rows_x, rows_c, activation, d_gate, d_up)
    summed = (
        lax.psum_scatter(
            term_gate.astype(jnp.float32).astype(jnp.bfloat16),
            "dp",
            scatter_dimension=0,
            tiled=True,
        ).astype(jnp.float32),
        lax.psum_scatter(
            term_up.astype(jnp.float32).astype(jnp.bfloat16), "dp", scatter_dimension=0, tiled=True
        ).astype(jnp.float32),
        lax.psum_scatter(
            term_down.astype(jnp.float32).astype(jnp.bfloat16),
            "dp",
            scatter_dimension=0,
            tiled=True,
        ).astype(jnp.float32),
    )
    grad_gate = summed[0].astype(jnp.bfloat16)
    grad_up = summed[1].astype(jnp.bfloat16)
    grad_down = summed[2].astype(jnp.bfloat16)
    returned = lax.all_to_all(
        part_rows.reshape(devices, CAP, model_width),
        "expert",
        split_axis=0,
        concat_axis=0,
        tiled=True,
    )
    combined = jnp.sum(
        returned.astype(jnp.float32).reshape(E_WIN, group_size, CAP, model_width), axis=1
    )
    grad_tokens = jnp.einsum(
        "kct,kcd->td", place_full, combined, precision=lax.Precision.HIGHEST
    ).astype(jnp.bfloat16)
    return (grad_tokens, grad_gate, grad_up, grad_down)


def solution(mesh):
    sizes = mesh.shape
    return jax.shard_map(
        kernel_body if sizes["expert"] == E_WIN and sizes["dp"] == 2 else body,
        mesh=mesh,
        in_specs=(
            P(("groups", "expert", "dp"), None),
            P(("groups", "expert", "dp"), None),
            P(("groups", "expert", "dp"), None),
            P(("groups", "expert", "dp"), None),
            P(("expert", "dp"), None),
            P(("expert", "dp"), None),
            P(("expert", "dp"), None),
        ),
        out_specs=(
            P(("groups", "expert", "dp"), None),
            P(("groups", "expert", "dp"), None),
            P(("groups", "expert", "dp"), None),
            P(("groups", "expert", "dp"), None),
        ),
        check_vma=False,
    )
```

```python
import functools

import jax
import jax.numpy as jnp
from jax import lax
from jax.experimental import pallas as pl
from jax.experimental.pallas import tpu as pltpu
from jax.sharding import PartitionSpec as P

E_WIN = 8
CAP = 4
FOLD = 4
BLOCK = FOLD * CAP
LAST = (((1,), (1,)), ((), ()))
FIRST = (((0,), (0,)), ((), ()))
F32 = jnp.float32
BF16 = jnp.bfloat16


def fold_columns(width):
    step = -(-width // (FOLD * 128)) * 128
    return [(j * step, min(width, (j + 1) * step)) for j in range(FOLD)]


def iota(shape, dim):
    return lax.broadcasted_iota(jnp.int32, shape, dim)


def dot(a, b):
    return jnp.dot(a, b, preferred_element_type=F32)


def exchange_kernel(
    experts, chunk,
    tok, cot, ids, route, gate_hbm, up_hbm, down_hbm,
    grad_tok, d_gate_out, d_up_out, act_out, x_out, c_out,
    gate_w, up_w, down_w, send_x, send_c, recv_x, recv_c, stage,
    gate_pre, up_pre, total, half_out, half_in, ret_out, ret_in,
    w_sem, xs_sem, xr_sem, cs_sem, cr_sem, xfs_sem, xfr_sem, cfs_sem, cfr_sem,
    half_sem, rs_sem, rr_sem,
):
    me = lax.axis_index("expert")
    core = lax.axis_index("dp")
    peer = 1 - core
    width, n_tok = tok.shape
    units = gate_hbm.shape[1]
    chunks = units // chunk
    cols = fold_columns(width)
    lines = experts * BLOCK
    own_rows = experts * CAP
    peer_id = {"dp": peer}

    barrier = pltpu.get_barrier_semaphore()
    for d in range(1, experts):
        pl.semaphore_signal(
            barrier, inc=1, device_id={"expert": lax.rem(me + d, experts)},
            device_id_type=pl.DeviceIdType.MESH,
        )
    pl.semaphore_signal(barrier, inc=1, device_id=peer_id, device_id_type=pl.DeviceIdType.MESH)

    def weight_copy(which, c):
        src = (gate_hbm, up_hbm, down_hbm)[which]
        dst = (gate_w, up_w, down_w)[which]
        rows = pl.ds(pl.multiple_of(c * chunk, chunk), chunk)
        return pltpu.make_async_copy(src.at[:, rows], dst.at[:, rows], w_sem.at[which, c])

    for which in range(3):
        for c in range(chunks):
            weight_copy(which, c).start()

    line = iota((lines, n_tok), 0)
    line_expert = line // BLOCK
    line_slot = (line % CAP).astype(F32)
    line_fold = (line // CAP) % FOLD
    member = jnp.zeros((lines, n_tok), F32)
    weight = jnp.zeros((lines, n_tok), F32)
    for p in range(ids.shape[0]):
        hit = ids[p : p + 1, :] == line_expert
        member += jnp.where(hit, 1.0, 0.0)
        weight += jnp.where(hit, route[p : p + 1, :], 0.0)
    earlier = jnp.where(iota((n_tok, n_tok), 0) < iota((n_tok, n_tok), 1), 1.0, 0.0)
    position = dot(member.astype(BF16), earlier.astype(BF16))
    place = jnp.where(position == line_slot, member, 0.0)
    slot_weight = jnp.sum(place * weight, axis=1, keepdims=True)
    picks = [jnp.where(line_fold == j, place, 0.0).astype(BF16) for j in range(FOLD)]

    def pack(selects, columns):
        full = columns(selects[0], *cols[0])
        for j in range(1, FOLD - 1):
            full += columns(selects[j], *cols[j])
        stage[...] = full
        lo, hi = cols[FOLD - 1]
        stage[:, : hi - lo] += columns(selects[FOLD - 1], lo, hi)
        return stage[...]

    def from_tokens(source):
        return lambda select, lo, hi: lax.dot_general(
            select, source[lo:hi, :], LAST, preferred_element_type=F32
        )

    def block(index):
        return pl.ds(pl.multiple_of(index * BLOCK, BLOCK), BLOCK)

    def slot(src):
        return block(core * experts + src)

    def row_send(send, recv, s_sem, r_sem, d):
        to = lax.rem(me + d, experts)
        return pltpu.make_async_remote_copy(
            src_ref=send.at[block(to)], dst_ref=recv.at[slot(me)],
            send_sem=s_sem.at[d], recv_sem=r_sem.at[d],
            device_id={"expert": to}, device_id_type=pl.DeviceIdType.MESH,
        )

    def row_arrival(send, recv, s_sem, r_sem, d):
        origin = lax.rem(me + experts - d, experts)
        return pltpu.make_async_remote_copy(
            src_ref=send.at[block(origin)], dst_ref=recv.at[slot(origin)],
            send_sem=s_sem.at[d], recv_sem=r_sem.at[d],
            device_id={"expert": origin}, device_id_type=pl.DeviceIdType.MESH,
        )

    def forward(recv, s_sem, r_sem, d):
        origin = lax.rem(me + experts - d, experts)
        return pltpu.make_async_remote_copy(
            src_ref=recv.at[slot(origin)], dst_ref=recv.at[slot(origin)],
            send_sem=s_sem.at[d], recv_sem=r_sem.at[d],
            device_id=peer_id, device_id_type=pl.DeviceIdType.MESH,
        )

    def forward_arrival(recv, s_sem, r_sem, d):
        origin = lax.rem(me + experts - d, experts)
        where = block(peer * experts + origin)
        return pltpu.make_async_remote_copy(
            src_ref=recv.at[where], dst_ref=recv.at[where],
            send_sem=s_sem.at[d], recv_sem=r_sem.at[d],
            device_id=peer_id, device_id_type=pl.DeviceIdType.MESH,
        )

    x_sems = (xs_sem, xr_sem)
    c_sems = (cs_sem, cr_sem)
    xf_sems = (xfs_sem, xfr_sem)
    cf_sems = (cfs_sem, cfr_sem)
    near_last = sorted(range(1, experts), key=lambda d: abs(2 * d - experts))

    send_x[...] = pack(picks, from_tokens(tok)).astype(BF16)
    recv_x[slot(me), :] = send_x[block(me), :]
    pl.semaphore_wait(barrier, experts)
    for d in near_last:
        row_send(send_x, recv_x, *x_sems, d).start()
    forward(recv_x, *xf_sems, 0).start()
    send_c[...] = (pack(picks, from_tokens(cot)) * slot_weight).astype(BF16)
    recv_c[slot(me), :] = send_c[block(me), :]
    for d in near_last:
        row_send(send_c, recv_c, *c_sems, d).start()
    forward(recv_c, *cf_sems, 0).start()

    all_rows = 2 * own_rows
    row = iota((all_rows, 2 * lines), 0)
    line_of = iota((all_rows, 2 * lines), 1)
    base = (row // CAP) * BLOCK + row % CAP

    def unpack(recv, out):
        for j, (lo, hi) in enumerate(cols):
            select = jnp.where(line_of == base + j * CAP, 1.0, 0.0).astype(BF16)
            out[:, lo:hi] = dot(select, recv[:, : hi - lo]).astype(BF16)

    def gather(send, recv, sems, f_sems, out):
        for d in near_last[::-1]:
            row_arrival(send, recv, *sems, d).wait_recv()
            forward(recv, *f_sems, d).start()
        for d in range(experts):
            forward_arrival(recv, *f_sems, d).wait_recv()
        unpack(recv, out)

    gather(send_x, recv_x, x_sems, xf_sems, x_out)

    def span(c):
        return pl.ds(pl.multiple_of(c * chunk, chunk), chunk)

    def project(c, carry):
        weight_copy(0, c).wait()
        weight_copy(1, c).wait()
        x = x_out[...]
        gate_pre[:, span(c)] = dot(x, gate_w[:, span(c)])
        up_pre[:, span(c)] = dot(x, up_w[:, span(c)])
        return carry

    lax.fori_loop(0, chunks, project, 0)
    gather(send_c, recv_c, c_sems, cf_sems, c_out)

    total[...] = jnp.zeros_like(total)

    def backward(c, carry):
        weight_copy(2, c).wait()
        d_act = dot(c_out[...], down_w[:, span(c)])
        gate = gate_pre[:, span(c)]
        up = up_pre[:, span(c)] + 1.0
        sig = jax.nn.sigmoid(1.702 * gate)
        gated = gate * sig
        act_out[:, span(c)] = (up * gated).astype(BF16)
        d_up = (d_act * gated).astype(BF16)
        d_gate = (d_act * up * (sig + 1.702 * gate * sig * (1.0 - sig))).astype(BF16)
        d_up_out[:, span(c)] = d_up
        d_gate_out[:, span(c)] = d_gate
        total[...] += lax.dot_general(
            d_gate, gate_w[:, span(c)], LAST, preferred_element_type=F32
        ) + lax.dot_general(d_up, up_w[:, span(c)], LAST, preferred_element_type=F32)
        return carry

    lax.fori_loop(0, chunks, backward, 0)

    def half_rows(which):
        return pl.ds(pl.multiple_of(which * own_rows, own_rows), own_rows)

    half_out[...] = total[half_rows(peer), :].astype(BF16)
    swap = pltpu.make_async_remote_copy(
        src_ref=half_out, dst_ref=half_in, send_sem=half_sem.at[0], recv_sem=half_sem.at[1],
        device_id=peer_id, device_id_type=pl.DeviceIdType.MESH,
    )
    swap.start()
    swap.wait()
    half_out[...] = (total[half_rows(core), :] + half_in[...].astype(F32)).astype(BF16)

    out_line = iota((lines, own_rows), 0)
    wanted = (out_line // BLOCK) * CAP + out_line % CAP
    matched = wanted == iota((lines, own_rows), 1)
    out_fold = (out_line // CAP) % FOLD
    puts = [
        jnp.where(jnp.logical_and(matched, out_fold == j), 1.0, 0.0).astype(BF16)
        for j in range(FOLD)
    ]
    ret_out[...] = pack(puts, lambda select, lo, hi: dot(select, half_out[:, lo:hi])).astype(BF16)
    ret_in[block(me), :] = ret_out[block(me), :]

    def ret_copy(d, sending):
        other = lax.rem(me + d, experts) if sending else lax.rem(me + experts - d, experts)
        return pltpu.make_async_remote_copy(
            src_ref=ret_out.at[block(other)], dst_ref=ret_in.at[block(me if sending else other)],
            send_sem=rs_sem.at[d], recv_sem=rr_sem.at[d],
            device_id={"expert": other}, device_id_type=pl.DeviceIdType.MESH,
        )

    for d in near_last:
        ret_copy(d, True).start()
    for d in range(1, experts):
        row_send(send_x, recv_x, *x_sems, d).wait_send()
        row_send(send_c, recv_c, *c_sems, d).wait_send()
    for d in range(experts):
        forward(recv_x, *xf_sems, d).wait_send()
        forward(recv_c, *cf_sems, d).wait_send()
    for d in range(1, experts):
        ret_copy(d, False).wait_recv()
    for j, (lo, hi) in enumerate(cols):
        grad_tok[lo:hi, :] = lax.dot_general(
            ret_in[:, : hi - lo], picks[j], FIRST, preferred_element_type=F32
        ).astype(BF16)
    for d in range(1, experts):
        ret_copy(d, True).wait_send()


def weight_kernel(d_gate, d_up, act, x, c, g_gate, g_up, g_down):
    def term(a, b):
        return lax.dot_general(a[...], b[...], FIRST, preferred_element_type=F32).astype(BF16)

    g_gate[...] = term(x, d_gate)
    g_up[...] = term(x, d_up)
    g_down[...] = term(c, act)


def kernel_body(tokens, cotangent, expert_ids, route_weight, gate_weight, up_weight, down_weight):
    experts = lax.axis_size("expert")
    n_tok, width = tokens.shape
    units = gate_weight.shape[0]
    chunk = 256
    rows = 2 * experts * CAP
    lines = experts * BLOCK
    lo, hi = fold_columns(width)[0]
    fold_width = hi - lo
    vmem = pl.BlockSpec(memory_space=pltpu.VMEM)
    hbm = pl.BlockSpec(memory_space=pl.ANY)
    sem = pltpu.SemaphoreType.DMA
    shape = jax.ShapeDtypeStruct
    grad_tokens, d_gate, d_up, act, x, c = pl.pallas_call(
        functools.partial(exchange_kernel, experts, chunk),
        out_shape=(
            shape((width, n_tok), BF16),
            shape((rows, units), BF16),
            shape((rows, units), BF16),
            shape((rows, units), BF16),
            shape((rows, width), BF16),
            shape((rows, width), BF16),
        ),
        in_specs=[vmem] * 4 + [hbm] * 3,
        out_specs=(vmem,) * 6,
        scratch_shapes=[
            pltpu.VMEM((width, units), BF16),
            pltpu.VMEM((width, units), BF16),
            pltpu.VMEM((width, units), BF16),
            pltpu.VMEM((lines, fold_width), BF16),
            pltpu.VMEM((lines, fold_width), BF16),
            pltpu.VMEM((2 * lines, fold_width), BF16),
            pltpu.VMEM((2 * lines, fold_width), BF16),
            pltpu.VMEM((lines, fold_width), F32),
            pltpu.VMEM((rows, units), F32),
            pltpu.VMEM((rows, units), F32),
            pltpu.VMEM((rows, width), F32),
            pltpu.VMEM((rows // 2, width), BF16),
            pltpu.VMEM((rows // 2, width), BF16),
            pltpu.VMEM((lines, fold_width), BF16),
            pltpu.VMEM((lines, fold_width), BF16),
            sem((3, units // chunk)),
            sem((experts,)), sem((experts,)), sem((experts,)), sem((experts,)),
            sem((experts,)), sem((experts,)), sem((experts,)), sem((experts,)),
            sem((2,)), sem((experts,)), sem((experts,)),
        ],
        compiler_params=pltpu.CompilerParams(
            collective_id=0, has_side_effects=True, vmem_limit_bytes=56 * 1024 * 1024
        ),
        name="exchange",
    )(
        tokens.T, cotangent.T, expert_ids.T, route_weight.T,
        gate_weight.T, up_weight.T, down_weight.T,
    )

    step = 384
    part = pl.BlockSpec((rows, step), lambda i: (0, i))
    whole = pl.BlockSpec((rows, units), lambda i: (0, 0))
    result = pl.BlockSpec((step, units), lambda i: (i, 0))
    grads = pl.pallas_call(
        weight_kernel,
        out_shape=(shape((width, units), BF16),) * 3,
        grid=(pl.cdiv(width, step),),
        in_specs=[whole, whole, whole, part, part],
        out_specs=(result,) * 3,
        compiler_params=pltpu.CompilerParams(vmem_limit_bytes=32 * 1024 * 1024),
        cost_estimate=pl.CostEstimate(
            flops=6 * rows * units * width, bytes_accessed=6 * units * width, transcendentals=0
        ),
        name="weight_grads",
    )(d_gate, d_up, act, x, c)
    return (grad_tokens.T, *(g.T for g in grads))


def expert_backward(rows_x, rows_c, w_gate, w_up, w_down):
    contract_last = (((1,), (1,)), ((), ()))
    gate_pre = lax.dot_general(rows_x, w_gate, contract_last, preferred_element_type=jnp.float32)
    up_pre = lax.dot_general(rows_x, w_up, contract_last, preferred_element_type=jnp.float32)
    d_act = lax.dot_general(rows_c, w_down, contract_last, preferred_element_type=jnp.float32)
    sigmoid_gate = jax.nn.sigmoid(1.702 * gate_pre)
    gated = gate_pre * sigmoid_gate
    activation = ((up_pre + 1.0) * gated).astype(jnp.bfloat16)
    d_up = (d_act * gated).astype(jnp.bfloat16)
    d_gate = (
        d_act
        * (up_pre + 1.0)
        * (sigmoid_gate + 1.702 * gate_pre * sigmoid_gate * (1.0 - sigmoid_gate))
    ).astype(jnp.bfloat16)
    partial_value = jnp.dot(d_gate, w_gate, preferred_element_type=jnp.float32) + jnp.dot(
        d_up, w_up, preferred_element_type=jnp.float32
    )
    return (activation, d_gate, d_up, partial_value)


def weight_terms(rows_x, rows_c, activation, d_gate, d_up):
    contract_first = (((0,), (0,)), ((), ()))
    term_gate = lax.dot_general(
        d_gate, rows_x, contract_first, preferred_element_type=jnp.float32
    ).astype(jnp.bfloat16)
    term_up = lax.dot_general(
        d_up, rows_x, contract_first, preferred_element_type=jnp.float32
    ).astype(jnp.bfloat16)
    term_down = lax.dot_general(
        activation, rows_c, contract_first, preferred_element_type=jnp.float32
    ).astype(jnp.bfloat16)
    return lax.optimization_barrier((term_gate, term_up, term_down))


def body(tokens, cotangent, expert_ids, route_weight, gate_weight, up_weight, down_weight):
    devices = lax.axis_size("expert")
    group_size = devices // E_WIN
    model_width = tokens.shape[1]
    window_ids = jnp.arange(E_WIN, dtype=jnp.int32)
    matches = expert_ids[:, :, None] == window_ids[None, None, :]
    member = jnp.any(matches, axis=1)
    weight_of = jnp.sum(jnp.where(matches, route_weight[:, :, None], 0.0), axis=1)
    position = jnp.cumsum(member.astype(jnp.int32), axis=0) - 1
    slot_ids = jnp.arange(CAP, dtype=jnp.int32)
    placement = jnp.logical_and(
        member.T[:, None, :], position.T[:, None, :] == slot_ids[None, :, None]
    )
    place_half = placement.astype(jnp.bfloat16)
    place_full = placement.astype(jnp.float32)
    picked_x = jnp.einsum(
        "kct,td->kcd", place_half, tokens, preferred_element_type=jnp.float32
    ).astype(jnp.bfloat16)
    picked_dy = jnp.einsum("kct,td->kcd", place_half, cotangent, preferred_element_type=jnp.float32)
    slot_weight = jnp.einsum("kct,tk->kc", place_full, weight_of, precision=lax.Precision.HIGHEST)
    picked_c = (slot_weight[:, :, None] * picked_dy).astype(jnp.bfloat16)
    send_x = jnp.repeat(picked_x, group_size, axis=0)
    send_c = jnp.repeat(picked_c, group_size, axis=0)
    recv_x, recv_c = (
        lax.all_to_all(send_x, "expert", split_axis=0, concat_axis=0, tiled=True),
        lax.all_to_all(send_c, "expert", split_axis=0, concat_axis=0, tiled=True),
    )
    rows_x = recv_x.reshape(devices * CAP, model_width)
    rows_c = recv_c.reshape(devices * CAP, model_width)
    full_gate, full_up, full_down = (
        lax.all_gather(gate_weight, "dp", axis=0, tiled=True),
        lax.all_gather(up_weight, "dp", axis=0, tiled=True),
        lax.all_gather(down_weight, "dp", axis=0, tiled=True),
    )
    activation, d_gate, d_up, partial_value = expert_backward(
        rows_x, rows_c, full_gate, full_up, full_down
    )
    part_rows = partial_value.astype(jnp.bfloat16)
    term_gate, term_up, term_down = weight_terms(rows_x, rows_c, activation, d_gate, d_up)
    summed = (
        lax.psum_scatter(
            term_gate.astype(jnp.float32).astype(jnp.bfloat16),
            "dp",
            scatter_dimension=0,
            tiled=True,
        ).astype(jnp.float32),
        lax.psum_scatter(
            term_up.astype(jnp.float32).astype(jnp.bfloat16), "dp", scatter_dimension=0, tiled=True
        ).astype(jnp.float32),
        lax.psum_scatter(
            term_down.astype(jnp.float32).astype(jnp.bfloat16),
            "dp",
            scatter_dimension=0,
            tiled=True,
        ).astype(jnp.float32),
    )
    grad_gate = summed[0].astype(jnp.bfloat16)
    grad_up = summed[1].astype(jnp.bfloat16)
    grad_down = summed[2].astype(jnp.bfloat16)
    returned = lax.all_to_all(
        part_rows.reshape(devices, CAP, model_width),
        "expert",
        split_axis=0,
        concat_axis=0,
        tiled=True,
    )
    combined = jnp.sum(
        returned.astype(jnp.float32).reshape(E_WIN, group_size, CAP, model_width), axis=1
    )
    grad_tokens = jnp.einsum(
        "kct,kcd->td", place_full, combined, precision=lax.Precision.HIGHEST
    ).astype(jnp.bfloat16)
    return (grad_tokens, grad_gate, grad_up, grad_down)


def solution(mesh):
    sizes = mesh.shape
    return jax.shard_map(
        kernel_body if sizes["expert"] == E_WIN and sizes["dp"] == 2 else body,
        mesh=mesh,
        in_specs=(
            P(("groups", "expert", "dp"), None),
            P(("groups", "expert", "dp"), None),
            P(("groups", "expert", "dp"), None),
            P(("groups", "expert", "dp"), None),
            P(("expert", "dp"), None),
            P(("expert", "dp"), None),
            P(("expert", "dp"), None),
        ),
        out_specs=(
            P(("groups", "expert", "dp"), None),
            P(("groups", "expert", "dp"), None),
            P(("groups", "expert", "dp"), None),
            P(("groups", "expert", "dp"), None),
        ),
        check_vma=False,
    )
```

```python
import functools

import jax
import jax.numpy as jnp
from jax import lax
from jax.experimental import pallas as pl
from jax.experimental.pallas import tpu as pltpu
from jax.sharding import PartitionSpec as P

E_WIN = 8
CAP = 4
FOLD = 4
BLOCK = FOLD * CAP
LAST = (((1,), (1,)), ((), ()))
FIRST = (((0,), (0,)), ((), ()))
F32 = jnp.float32
BF16 = jnp.bfloat16


def fold_columns(width):
    step = -(-width // (FOLD * 128)) * 128
    return [(j * step, min(width, (j + 1) * step)) for j in range(FOLD)]


def iota(shape, dim):
    return lax.broadcasted_iota(jnp.int32, shape, dim)


def dot(a, b):
    return jnp.dot(a, b, preferred_element_type=F32)


def exchange_kernel(
    experts, chunk,
    tok, cot, ids, route, gate_hbm, up_hbm, down_hbm,
    grad_tok, d_gate_out, d_up_out, act_out, x_out, c_out,
    gate_w, up_w, down_w, send_x, send_c, recv_x, recv_c, stage,
    gate_pre, up_pre, total, half_out, half_in, ret_out, ret_in,
    w_sem, xs_sem, xr_sem, cs_sem, cr_sem, xfs_sem, xfr_sem, cfs_sem, cfr_sem,
    half_sem, rs_sem, rr_sem,
):
    me = lax.axis_index("expert")
    core = lax.axis_index("dp")
    peer = 1 - core
    width, n_tok = tok.shape
    units = gate_hbm.shape[1]
    chunks = units // chunk
    cols = fold_columns(width)
    lines = experts * BLOCK
    own_rows = experts * CAP
    peer_id = {"dp": peer}

    barrier = pltpu.get_barrier_semaphore()
    for d in range(1, experts):
        pl.semaphore_signal(
            barrier, inc=1, device_id={"expert": lax.rem(me + d, experts)},
            device_id_type=pl.DeviceIdType.MESH,
        )
    pl.semaphore_signal(barrier, inc=1, device_id=peer_id, device_id_type=pl.DeviceIdType.MESH)

    def weight_copy(which, c):
        src = (gate_hbm, up_hbm, down_hbm)[which]
        dst = (gate_w, up_w, down_w)[which]
        rows = pl.ds(pl.multiple_of(c * chunk, chunk), chunk)
        return pltpu.make_async_copy(src.at[:, rows], dst.at[:, rows], w_sem.at[which, c])

    for which in range(3):
        for c in range(chunks):
            weight_copy(which, c).start()

    line = iota((lines, n_tok), 0)
    line_expert = line // BLOCK
    line_slot = (line % CAP).astype(F32)
    line_fold = (line // CAP) % FOLD
    member = jnp.zeros((lines, n_tok), F32)
    weight = jnp.zeros((lines, n_tok), F32)
    for p in range(ids.shape[0]):
        hit = ids[p : p + 1, :] == line_expert
        member += jnp.where(hit, 1.0, 0.0)
        weight += jnp.where(hit, route[p : p + 1, :], 0.0)
    earlier = jnp.where(iota((n_tok, n_tok), 0) < iota((n_tok, n_tok), 1), 1.0, 0.0)
    position = dot(member.astype(BF16), earlier.astype(BF16))
    place = jnp.where(position == line_slot, member, 0.0)
    slot_weight = jnp.sum(place * weight, axis=1, keepdims=True)
    picks = [jnp.where(line_fold == j, place, 0.0).astype(BF16) for j in range(FOLD)]

    def pack(selects, columns):
        full = columns(selects[0], *cols[0])
        for j in range(1, FOLD - 1):
            full += columns(selects[j], *cols[j])
        stage[...] = full
        lo, hi = cols[FOLD - 1]
        stage[:, : hi - lo] += columns(selects[FOLD - 1], lo, hi)
        return stage[...]

    def from_tokens(source):
        return lambda select, lo, hi: lax.dot_general(
            select, source[lo:hi, :], LAST, preferred_element_type=F32
        )

    def block(index):
        return pl.ds(pl.multiple_of(index * BLOCK, BLOCK), BLOCK)

    def slot(src):
        return block(core * experts + src)

    def row_send(send, recv, s_sem, r_sem, d):
        to = lax.rem(me + d, experts)
        return pltpu.make_async_remote_copy(
            src_ref=send.at[block(to)], dst_ref=recv.at[slot(me)],
            send_sem=s_sem.at[d], recv_sem=r_sem.at[d],
            device_id={"expert": to}, device_id_type=pl.DeviceIdType.MESH,
        )

    def row_arrival(send, recv, s_sem, r_sem, d):
        origin = lax.rem(me + experts - d, experts)
        return pltpu.make_async_remote_copy(
            src_ref=send.at[block(origin)], dst_ref=recv.at[slot(origin)],
            send_sem=s_sem.at[d], recv_sem=r_sem.at[d],
            device_id={"expert": origin}, device_id_type=pl.DeviceIdType.MESH,
        )

    def forward(recv, s_sem, r_sem, d):
        origin = lax.rem(me + experts - d, experts)
        return pltpu.make_async_remote_copy(
            src_ref=recv.at[slot(origin)], dst_ref=recv.at[slot(origin)],
            send_sem=s_sem.at[d], recv_sem=r_sem.at[d],
            device_id=peer_id, device_id_type=pl.DeviceIdType.MESH,
        )

    def forward_arrival(recv, s_sem, r_sem, d):
        origin = lax.rem(me + experts - d, experts)
        where = block(peer * experts + origin)
        return pltpu.make_async_remote_copy(
            src_ref=recv.at[where], dst_ref=recv.at[where],
            send_sem=s_sem.at[d], recv_sem=r_sem.at[d],
            device_id=peer_id, device_id_type=pl.DeviceIdType.MESH,
        )

    x_sems = (xs_sem, xr_sem)
    c_sems = (cs_sem, cr_sem)
    xf_sems = (xfs_sem, xfr_sem)
    cf_sems = (cfs_sem, cfr_sem)
    near_last = sorted(range(1, experts), key=lambda d: abs(2 * d - experts))

    send_x[...] = pack(picks, from_tokens(tok)).astype(BF16)
    recv_x[slot(me), :] = send_x[block(me), :]
    pl.semaphore_wait(barrier, experts)
    for d in near_last:
        row_send(send_x, recv_x, *x_sems, d).start()
    forward(recv_x, *xf_sems, 0).start()
    send_c[...] = (pack(picks, from_tokens(cot)) * slot_weight).astype(BF16)
    recv_c[slot(me), :] = send_c[block(me), :]
    for d in near_last:
        row_send(send_c, recv_c, *c_sems, d).start()
    forward(recv_c, *cf_sems, 0).start()

    all_rows = 2 * own_rows
    row = iota((all_rows, 2 * lines), 0)
    line_of = iota((all_rows, 2 * lines), 1)
    base = (row // CAP) * BLOCK + row % CAP

    def unpack(recv, out):
        for j, (lo, hi) in enumerate(cols):
            select = jnp.where(line_of == base + j * CAP, 1.0, 0.0).astype(BF16)
            out[:, lo:hi] = dot(select, recv[:, : hi - lo]).astype(BF16)

    def gather(send, recv, sems, f_sems, out):
        for d in near_last[::-1]:
            row_arrival(send, recv, *sems, d).wait_recv()
            forward(recv, *f_sems, d).start()
        for d in range(experts):
            forward_arrival(recv, *f_sems, d).wait_recv()
        unpack(recv, out)

    gather(send_x, recv_x, x_sems, xf_sems, x_out)

    def span(c):
        return pl.ds(pl.multiple_of(c * chunk, chunk), chunk)

    def project(c, carry):
        weight_copy(0, c).wait()
        weight_copy(1, c).wait()
        x = x_out[...]
        gate_pre[:, span(c)] = dot(x, gate_w[:, span(c)])
        up_pre[:, span(c)] = dot(x, up_w[:, span(c)])
        return carry

    lax.fori_loop(0, chunks, project, 0)
    gather(send_c, recv_c, c_sems, cf_sems, c_out)

    total[...] = jnp.zeros_like(total)

    def backward(c, carry):
        weight_copy(2, c).wait()
        d_act = dot(c_out[...], down_w[:, span(c)])
        gate = gate_pre[:, span(c)]
        up = up_pre[:, span(c)] + 1.0
        sig = jax.nn.sigmoid(1.702 * gate)
        gated = gate * sig
        act_out[:, span(c)] = (up * gated).astype(BF16)
        d_up = (d_act * gated).astype(BF16)
        d_gate = (d_act * up * (sig + 1.702 * gate * sig * (1.0 - sig))).astype(BF16)
        d_up_out[:, span(c)] = d_up
        d_gate_out[:, span(c)] = d_gate
        total[...] += lax.dot_general(
            d_gate, gate_w[:, span(c)], LAST, preferred_element_type=F32
        ) + lax.dot_general(d_up, up_w[:, span(c)], LAST, preferred_element_type=F32)
        return carry

    lax.fori_loop(0, chunks, backward, 0)

    def half_rows(which):
        return pl.ds(pl.multiple_of(which * own_rows, own_rows), own_rows)

    half_out[...] = total[half_rows(peer), :].astype(BF16)
    swap = pltpu.make_async_remote_copy(
        src_ref=half_out, dst_ref=half_in, send_sem=half_sem.at[0], recv_sem=half_sem.at[1],
        device_id=peer_id, device_id_type=pl.DeviceIdType.MESH,
    )
    swap.start()
    swap.wait()
    half_out[...] = (total[half_rows(core), :] + half_in[...].astype(F32)).astype(BF16)

    out_line = iota((lines, own_rows), 0)
    wanted = (out_line // BLOCK) * CAP + out_line % CAP
    matched = wanted == iota((lines, own_rows), 1)
    out_fold = (out_line // CAP) % FOLD
    puts = [
        jnp.where(jnp.logical_and(matched, out_fold == j), 1.0, 0.0).astype(BF16)
        for j in range(FOLD)
    ]
    ret_out[...] = pack(puts, lambda select, lo, hi: dot(select, half_out[:, lo:hi])).astype(BF16)
    ret_in[block(me), :] = ret_out[block(me), :]

    def ret_copy(d, sending):
        other = lax.rem(me + d, experts) if sending else lax.rem(me + experts - d, experts)
        return pltpu.make_async_remote_copy(
            src_ref=ret_out.at[block(other)], dst_ref=ret_in.at[block(me if sending else other)],
            send_sem=rs_sem.at[d], recv_sem=rr_sem.at[d],
            device_id={"expert": other}, device_id_type=pl.DeviceIdType.MESH,
        )

    for d in near_last:
        ret_copy(d, True).start()
    for d in range(1, experts):
        row_send(send_x, recv_x, *x_sems, d).wait_send()
        row_send(send_c, recv_c, *c_sems, d).wait_send()
    for d in range(experts):
        forward(recv_x, *xf_sems, d).wait_send()
        forward(recv_c, *cf_sems, d).wait_send()
    for d in range(1, experts):
        ret_copy(d, False).wait_recv()
    for j, (lo, hi) in enumerate(cols):
        grad_tok[lo:hi, :] = lax.dot_general(
            ret_in[:, : hi - lo], picks[j], FIRST, preferred_element_type=F32
        ).astype(BF16)
    for d in range(1, experts):
        ret_copy(d, True).wait_send()


def weight_kernel(d_gate, d_up, act, x, c, g_gate, g_up, g_down):
    def term(a, b):
        return lax.dot_general(a[...], b[...], FIRST, preferred_element_type=F32).astype(BF16)

    g_gate[...] = term(x, d_gate)
    g_up[...] = term(x, d_up)
    g_down[...] = term(c, act)


def kernel_body(tokens, cotangent, expert_ids, route_weight, gate_weight, up_weight, down_weight):
    experts = lax.axis_size("expert")
    n_tok, width = tokens.shape
    units = gate_weight.shape[0]
    chunk = 256
    rows = 2 * experts * CAP
    lines = experts * BLOCK
    lo, hi = fold_columns(width)[0]
    fold_width = hi - lo
    vmem = pl.BlockSpec(memory_space=pltpu.VMEM)
    hbm = pl.BlockSpec(memory_space=pl.ANY)
    sem = pltpu.SemaphoreType.DMA
    shape = jax.ShapeDtypeStruct
    grad_tokens, d_gate, d_up, act, x, c = pl.pallas_call(
        functools.partial(exchange_kernel, experts, chunk),
        out_shape=(
            shape((width, n_tok), BF16),
            shape((rows, units), BF16),
            shape((rows, units), BF16),
            shape((rows, units), BF16),
            shape((rows, width), BF16),
            shape((rows, width), BF16),
        ),
        in_specs=[vmem] * 4 + [hbm] * 3,
        out_specs=(vmem,) * 6,
        scratch_shapes=[
            pltpu.VMEM((width, units), BF16),
            pltpu.VMEM((width, units), BF16),
            pltpu.VMEM((width, units), BF16),
            pltpu.VMEM((lines, fold_width), BF16),
            pltpu.VMEM((lines, fold_width), BF16),
            pltpu.VMEM((2 * lines, fold_width), BF16),
            pltpu.VMEM((2 * lines, fold_width), BF16),
            pltpu.VMEM((lines, fold_width), F32),
            pltpu.VMEM((rows, units), F32),
            pltpu.VMEM((rows, units), F32),
            pltpu.VMEM((rows, width), F32),
            pltpu.VMEM((rows // 2, width), BF16),
            pltpu.VMEM((rows // 2, width), BF16),
            pltpu.VMEM((lines, fold_width), BF16),
            pltpu.VMEM((lines, fold_width), BF16),
            sem((3, units // chunk)),
            sem((experts,)), sem((experts,)), sem((experts,)), sem((experts,)),
            sem((experts,)), sem((experts,)), sem((experts,)), sem((experts,)),
            sem((2,)), sem((experts,)), sem((experts,)),
        ],
        compiler_params=pltpu.CompilerParams(
            collective_id=0, has_side_effects=True, vmem_limit_bytes=56 * 1024 * 1024
        ),
        name="exchange",
    )(
        tokens.T, cotangent.T, expert_ids.T, route_weight.T,
        gate_weight.T, up_weight.T, down_weight.T,
    )

    step = 384
    part = pl.BlockSpec((rows, step), lambda i: (0, i))
    whole = pl.BlockSpec((rows, units), lambda i: (0, 0))
    result = pl.BlockSpec((step, units), lambda i: (i, 0))
    grads = pl.pallas_call(
        weight_kernel,
        out_shape=(shape((width, units), BF16),) * 3,
        grid=(pl.cdiv(width, step),),
        in_specs=[whole, whole, whole, part, part],
        out_specs=(result,) * 3,
        compiler_params=pltpu.CompilerParams(vmem_limit_bytes=56 * 1024 * 1024),
        cost_estimate=pl.CostEstimate(
            flops=6 * rows * units * width, bytes_accessed=6 * units * width, transcendentals=0
        ),
        name="weight_grads",
    )(d_gate, d_up, act, x, c)
    return (grad_tokens.T, *(g.T for g in grads))


def expert_backward(rows_x, rows_c, w_gate, w_up, w_down):
    contract_last = (((1,), (1,)), ((), ()))
    gate_pre = lax.dot_general(rows_x, w_gate, contract_last, preferred_element_type=jnp.float32)
    up_pre = lax.dot_general(rows_x, w_up, contract_last, preferred_element_type=jnp.float32)
    d_act = lax.dot_general(rows_c, w_down, contract_last, preferred_element_type=jnp.float32)
    sigmoid_gate = jax.nn.sigmoid(1.702 * gate_pre)
    gated = gate_pre * sigmoid_gate
    activation = ((up_pre + 1.0) * gated).astype(jnp.bfloat16)
    d_up = (d_act * gated).astype(jnp.bfloat16)
    d_gate = (
        d_act
        * (up_pre + 1.0)
        * (sigmoid_gate + 1.702 * gate_pre * sigmoid_gate * (1.0 - sigmoid_gate))
    ).astype(jnp.bfloat16)
    partial_value = jnp.dot(d_gate, w_gate, preferred_element_type=jnp.float32) + jnp.dot(
        d_up, w_up, preferred_element_type=jnp.float32
    )
    return (activation, d_gate, d_up, partial_value)


def weight_terms(rows_x, rows_c, activation, d_gate, d_up):
    contract_first = (((0,), (0,)), ((), ()))
    term_gate = lax.dot_general(
        d_gate, rows_x, contract_first, preferred_element_type=jnp.float32
    ).astype(jnp.bfloat16)
    term_up = lax.dot_general(
        d_up, rows_x, contract_first, preferred_element_type=jnp.float32
    ).astype(jnp.bfloat16)
    term_down = lax.dot_general(
        activation, rows_c, contract_first, preferred_element_type=jnp.float32
    ).astype(jnp.bfloat16)
    return lax.optimization_barrier((term_gate, term_up, term_down))


def body(tokens, cotangent, expert_ids, route_weight, gate_weight, up_weight, down_weight):
    devices = lax.axis_size("expert")
    group_size = devices // E_WIN
    model_width = tokens.shape[1]
    window_ids = jnp.arange(E_WIN, dtype=jnp.int32)
    matches = expert_ids[:, :, None] == window_ids[None, None, :]
    member = jnp.any(matches, axis=1)
    weight_of = jnp.sum(jnp.where(matches, route_weight[:, :, None], 0.0), axis=1)
    position = jnp.cumsum(member.astype(jnp.int32), axis=0) - 1
    slot_ids = jnp.arange(CAP, dtype=jnp.int32)
    placement = jnp.logical_and(
        member.T[:, None, :], position.T[:, None, :] == slot_ids[None, :, None]
    )
    place_half = placement.astype(jnp.bfloat16)
    place_full = placement.astype(jnp.float32)
    picked_x = jnp.einsum(
        "kct,td->kcd", place_half, tokens, preferred_element_type=jnp.float32
    ).astype(jnp.bfloat16)
    picked_dy = jnp.einsum("kct,td->kcd", place_half, cotangent, preferred_element_type=jnp.float32)
    slot_weight = jnp.einsum("kct,tk->kc", place_full, weight_of, precision=lax.Precision.HIGHEST)
    picked_c = (slot_weight[:, :, None] * picked_dy).astype(jnp.bfloat16)
    send_x = jnp.repeat(picked_x, group_size, axis=0)
    send_c = jnp.repeat(picked_c, group_size, axis=0)
    recv_x, recv_c = (
        lax.all_to_all(send_x, "expert", split_axis=0, concat_axis=0, tiled=True),
        lax.all_to_all(send_c, "expert", split_axis=0, concat_axis=0, tiled=True),
    )
    rows_x = recv_x.reshape(devices * CAP, model_width)
    rows_c = recv_c.reshape(devices * CAP, model_width)
    full_gate, full_up, full_down = (
        lax.all_gather(gate_weight, "dp", axis=0, tiled=True),
        lax.all_gather(up_weight, "dp", axis=0, tiled=True),
        lax.all_gather(down_weight, "dp", axis=0, tiled=True),
    )
    activation, d_gate, d_up, partial_value = expert_backward(
        rows_x, rows_c, full_gate, full_up, full_down
    )
    part_rows = partial_value.astype(jnp.bfloat16)
    term_gate, term_up, term_down = weight_terms(rows_x, rows_c, activation, d_gate, d_up)
    summed = (
        lax.psum_scatter(
            term_gate.astype(jnp.float32).astype(jnp.bfloat16),
            "dp",
            scatter_dimension=0,
            tiled=True,
        ).astype(jnp.float32),
        lax.psum_scatter(
            term_up.astype(jnp.float32).astype(jnp.bfloat16), "dp", scatter_dimension=0, tiled=True
        ).astype(jnp.float32),
        lax.psum_scatter(
            term_down.astype(jnp.float32).astype(jnp.bfloat16),
            "dp",
            scatter_dimension=0,
            tiled=True,
        ).astype(jnp.float32),
    )
    grad_gate = summed[0].astype(jnp.bfloat16)
    grad_up = summed[1].astype(jnp.bfloat16)
    grad_down = summed[2].astype(jnp.bfloat16)
    returned = lax.all_to_all(
        part_rows.reshape(devices, CAP, model_width),
        "expert",
        split_axis=0,
        concat_axis=0,
        tiled=True,
    )
    combined = jnp.sum(
        returned.astype(jnp.float32).reshape(E_WIN, group_size, CAP, model_width), axis=1
    )
    grad_tokens = jnp.einsum(
        "kct,kcd->td", place_full, combined, precision=lax.Precision.HIGHEST
    ).astype(jnp.bfloat16)
    return (grad_tokens, grad_gate, grad_up, grad_down)


def solution(mesh):
    sizes = mesh.shape
    return jax.shard_map(
        kernel_body if sizes["expert"] == E_WIN and sizes["dp"] == 2 else body,
        mesh=mesh,
        in_specs=(
            P(("groups", "expert", "dp"), None),
            P(("groups", "expert", "dp"), None),
            P(("groups", "expert", "dp"), None),
            P(("groups", "expert", "dp"), None),
            P(("expert", "dp"), None),
            P(("expert", "dp"), None),
            P(("expert", "dp"), None),
        ),
        out_specs=(
            P(("groups", "expert", "dp"), None),
            P(("groups", "expert", "dp"), None),
            P(("groups", "expert", "dp"), None),
            P(("groups", "expert", "dp"), None),
        ),
        check_vma=False,
    )
```

```python
import functools

import jax
import jax.numpy as jnp
from jax import lax
from jax.experimental import pallas as pl
from jax.experimental.pallas import tpu as pltpu
from jax.sharding import PartitionSpec as P

E_WIN = 8
CAP = 4
FOLD = 4
BLOCK = FOLD * CAP
LAST = (((1,), (1,)), ((), ()))
FIRST = (((0,), (0,)), ((), ()))
F32 = jnp.float32
BF16 = jnp.bfloat16


def fold_columns(width):
    step = -(-width // (FOLD * 128)) * 128
    return [(j * step, min(width, (j + 1) * step)) for j in range(FOLD)]


def iota(shape, dim):
    return lax.broadcasted_iota(jnp.int32, shape, dim)


def dot(a, b):
    return jnp.dot(a, b, preferred_element_type=F32)


def exchange_kernel(
    experts, chunk,
    tok, cot, ids, route, gate_hbm, up_hbm, down_hbm,
    ret_in, place_out, d_gate_out, d_up_out, act_out, x_out, c_out,
    gate_w, up_w, down_w, send_x, send_c, recv_x, recv_c, stage,
    gate_pre, up_pre, total, half_out, half_in, ret_out,
    w_sem, xs_sem, xr_sem, cs_sem, cr_sem, xfs_sem, xfr_sem, cfs_sem, cfr_sem,
    half_sem, rs_sem, rr_sem,
):
    me = lax.axis_index("expert")
    core = lax.axis_index("dp")
    peer = 1 - core
    width, n_tok = tok.shape
    units = gate_hbm.shape[1]
    chunks = units // chunk
    cols = fold_columns(width)
    lines = experts * BLOCK
    own_rows = experts * CAP
    peer_id = {"dp": peer}

    barrier = pltpu.get_barrier_semaphore()
    for d in range(1, experts):
        pl.semaphore_signal(
            barrier, inc=1, device_id={"expert": lax.rem(me + d, experts)},
            device_id_type=pl.DeviceIdType.MESH,
        )
    pl.semaphore_signal(barrier, inc=1, device_id=peer_id, device_id_type=pl.DeviceIdType.MESH)

    def weight_copy(which, c):
        src = (gate_hbm, up_hbm, down_hbm)[which]
        dst = (gate_w, up_w, down_w)[which]
        rows = pl.ds(c * chunk if isinstance(c, int) else pl.multiple_of(c * chunk, chunk), chunk)
        return pltpu.make_async_copy(src.at[:, rows], dst.at[:, rows], w_sem.at[which, c])

    for which in range(3):
        for c in range(chunks):
            weight_copy(which, c).start()

    line = iota((lines, n_tok), 0)
    line_expert = line // BLOCK
    line_slot = (line % CAP).astype(F32)
    line_fold = (line // CAP) % FOLD
    member = jnp.zeros((lines, n_tok), F32)
    weight = jnp.zeros((lines, n_tok), F32)
    for p in range(ids.shape[0]):
        hit = ids[p : p + 1, :] == line_expert
        member += jnp.where(hit, 1.0, 0.0)
        weight += jnp.where(hit, route[p : p + 1, :], 0.0)
    earlier = jnp.where(iota((n_tok, n_tok), 0) < iota((n_tok, n_tok), 1), 1.0, 0.0)
    position = dot(member.astype(BF16), earlier.astype(BF16))
    place = jnp.where(position == line_slot, member, 0.0)
    place_out[...] = place.astype(BF16)
    slot_weight = jnp.sum(place * weight, axis=1, keepdims=True)
    picks = [jnp.where(line_fold == j, place, 0.0).astype(BF16) for j in range(FOLD)]

    def pack(selects, columns):
        full = columns(selects[0], *cols[0])
        for j in range(1, FOLD - 1):
            full += columns(selects[j], *cols[j])
        stage[...] = full
        lo, hi = cols[FOLD - 1]
        stage[:, : hi - lo] += columns(selects[FOLD - 1], lo, hi)
        return stage[...]

    def from_tokens(source):
        return lambda select, lo, hi: lax.dot_general(
            select, source[lo:hi, :], LAST, preferred_element_type=F32
        )

    def block(index):
        return pl.ds(pl.multiple_of(index * BLOCK, BLOCK), BLOCK)

    def slot(src):
        return block(core * experts + src)

    def row_send(send, recv, s_sem, r_sem, d):
        to = lax.rem(me + d, experts)
        return pltpu.make_async_remote_copy(
            src_ref=send.at[block(to)], dst_ref=recv.at[slot(me)],
            send_sem=s_sem.at[d], recv_sem=r_sem.at[d],
            device_id={"expert": to}, device_id_type=pl.DeviceIdType.MESH,
        )

    def row_arrival(send, recv, s_sem, r_sem, d):
        origin = lax.rem(me + experts - d, experts)
        return pltpu.make_async_remote_copy(
            src_ref=send.at[block(origin)], dst_ref=recv.at[slot(origin)],
            send_sem=s_sem.at[d], recv_sem=r_sem.at[d],
            device_id={"expert": origin}, device_id_type=pl.DeviceIdType.MESH,
        )

    def forward(recv, s_sem, r_sem, d):
        origin = lax.rem(me + experts - d, experts)
        return pltpu.make_async_remote_copy(
            src_ref=recv.at[slot(origin)], dst_ref=recv.at[slot(origin)],
            send_sem=s_sem.at[d], recv_sem=r_sem.at[d],
            device_id=peer_id, device_id_type=pl.DeviceIdType.MESH,
        )

    def forward_arrival(recv, s_sem, r_sem, d):
        origin = lax.rem(me + experts - d, experts)
        where = block(peer * experts + origin)
        return pltpu.make_async_remote_copy(
            src_ref=recv.at[where], dst_ref=recv.at[where],
            send_sem=s_sem.at[d], recv_sem=r_sem.at[d],
            device_id=peer_id, device_id_type=pl.DeviceIdType.MESH,
        )

    x_sems = (xs_sem, xr_sem)
    c_sems = (cs_sem, cr_sem)
    xf_sems = (xfs_sem, xfr_sem)
    cf_sems = (cfs_sem, cfr_sem)
    near_last = sorted(range(1, experts), key=lambda d: abs(2 * d - experts))

    send_x[...] = pack(picks, from_tokens(tok)).astype(BF16)
    recv_x[slot(me), :] = send_x[block(me), :]
    pl.semaphore_wait(barrier, experts)
    for d in near_last:
        row_send(send_x, recv_x, *x_sems, d).start()
    forward(recv_x, *xf_sems, 0).start()
    send_c[...] = (pack(picks, from_tokens(cot)) * slot_weight).astype(BF16)
    recv_c[slot(me), :] = send_c[block(me), :]
    for d in near_last:
        row_send(send_c, recv_c, *c_sems, d).start()
    forward(recv_c, *cf_sems, 0).start()

    all_rows = 2 * own_rows
    row = iota((all_rows, 2 * lines), 0)
    line_of = iota((all_rows, 2 * lines), 1)
    base = (row // CAP) * BLOCK + row % CAP

    def unpack(recv, out):
        for j, (lo, hi) in enumerate(cols):
            select = jnp.where(line_of == base + j * CAP, 1.0, 0.0).astype(BF16)
            out[:, lo:hi] = dot(select, recv[:, : hi - lo]).astype(BF16)

    def relay(send, recv, sems, f_sems, steps):
        for d in steps:
            row_arrival(send, recv, *sems, d).wait_recv()
            forward(recv, *f_sems, d).start()

    def finish(recv, f_sems, out):
        for d in range(experts):
            forward_arrival(recv, *f_sems, d).wait_recv()
        unpack(recv, out)

    arrivals = near_last[::-1]
    relay(send_x, recv_x, x_sems, xf_sems, arrivals)
    finish(recv_x, xf_sems, x_out)

    def span(c):
        return pl.ds(c * chunk if isinstance(c, int) else pl.multiple_of(c * chunk, chunk), chunk)

    def project(c):
        weight_copy(0, c).wait()
        weight_copy(1, c).wait()
        x = x_out[...]
        gate_pre[:, span(c)] = dot(x, gate_w[:, span(c)])
        up_pre[:, span(c)] = dot(x, up_w[:, span(c)])

    share = -(-len(arrivals) // chunks)
    for c in range(chunks):
        project(c)
        relay(send_c, recv_c, c_sems, cf_sems, arrivals[c * share : (c + 1) * share])
    finish(recv_c, cf_sems, c_out)

    total[...] = jnp.zeros_like(total)

    def backward(c, carry):
        weight_copy(2, c).wait()
        d_act = dot(c_out[...], down_w[:, span(c)])
        gate = gate_pre[:, span(c)]
        up = up_pre[:, span(c)] + 1.0
        sig = jax.nn.sigmoid(1.702 * gate)
        gated = gate * sig
        act_out[:, span(c)] = (up * gated).astype(BF16)
        d_up = (d_act * gated).astype(BF16)
        d_gate = (d_act * up * (sig + 1.702 * gate * sig * (1.0 - sig))).astype(BF16)
        d_up_out[:, span(c)] = d_up
        d_gate_out[:, span(c)] = d_gate
        total[...] += lax.dot_general(
            d_gate, gate_w[:, span(c)], LAST, preferred_element_type=F32
        ) + lax.dot_general(d_up, up_w[:, span(c)], LAST, preferred_element_type=F32)
        return carry

    lax.fori_loop(0, chunks, backward, 0)

    def half_rows(which):
        return pl.ds(pl.multiple_of(which * own_rows, own_rows), own_rows)

    half_out[...] = total[half_rows(peer), :].astype(BF16)
    swap = pltpu.make_async_remote_copy(
        src_ref=half_out, dst_ref=half_in, send_sem=half_sem.at[0], recv_sem=half_sem.at[1],
        device_id=peer_id, device_id_type=pl.DeviceIdType.MESH,
    )
    swap.start()
    swap.wait()
    half_out[...] = (total[half_rows(core), :] + half_in[...].astype(F32)).astype(BF16)

    out_line = iota((lines, own_rows), 0)
    wanted = (out_line // BLOCK) * CAP + out_line % CAP
    matched = wanted == iota((lines, own_rows), 1)
    out_fold = (out_line // CAP) % FOLD
    puts = [
        jnp.where(jnp.logical_and(matched, out_fold == j), 1.0, 0.0).astype(BF16)
        for j in range(FOLD)
    ]
    ret_out[...] = pack(puts, lambda select, lo, hi: dot(select, half_out[:, lo:hi])).astype(BF16)
    ret_in[block(me), :] = ret_out[block(me), :]

    def ret_copy(d, sending):
        other = lax.rem(me + d, experts) if sending else lax.rem(me + experts - d, experts)
        return pltpu.make_async_remote_copy(
            src_ref=ret_out.at[block(other)], dst_ref=ret_in.at[block(me if sending else other)],
            send_sem=rs_sem.at[d], recv_sem=rr_sem.at[d],
            device_id={"expert": other}, device_id_type=pl.DeviceIdType.MESH,
        )

    for d in near_last:
        ret_copy(d, True).start()
    for d in range(1, experts):
        row_send(send_x, recv_x, *x_sems, d).wait_send()
        row_send(send_c, recv_c, *c_sems, d).wait_send()
    for d in range(experts):
        forward(recv_x, *xf_sems, d).wait_send()
        forward(recv_c, *cf_sems, d).wait_send()
    for d in range(1, experts):
        ret_copy(d, False).wait_recv()
    for d in range(1, experts):
        ret_copy(d, True).wait_send()


def weight_kernel(per_fold, d_gate, d_up, act, x, c, ret, place, g_tok, g_gate, g_up, g_down):
    fold = pl.program_id(0) // per_fold
    line_fold = (iota(place.shape, 0) // CAP) % FOLD
    take = jnp.where(line_fold == fold, place[...].astype(F32), 0.0).astype(BF16)
    g_tok[...] = lax.dot_general(ret[...], take, FIRST, preferred_element_type=F32).astype(BF16)

    def term(a, b):
        return lax.dot_general(a[...], b[...], FIRST, preferred_element_type=F32).astype(BF16)

    g_gate[...] = term(x, d_gate)
    g_up[...] = term(x, d_up)
    g_down[...] = term(c, act)


def kernel_body(tokens, cotangent, expert_ids, route_weight, gate_weight, up_weight, down_weight):
    experts = lax.axis_size("expert")
    n_tok, width = tokens.shape
    units = gate_weight.shape[0]
    chunk = 256
    rows = 2 * experts * CAP
    lines = experts * BLOCK
    lo, hi = fold_columns(width)[0]
    fold_width = hi - lo
    vmem = pl.BlockSpec(memory_space=pltpu.VMEM)
    hbm = pl.BlockSpec(memory_space=pl.ANY)
    sem = pltpu.SemaphoreType.DMA
    shape = jax.ShapeDtypeStruct
    ret, place, d_gate, d_up, act, x, c = pl.pallas_call(
        functools.partial(exchange_kernel, experts, chunk),
        out_shape=(
            shape((lines, fold_width), BF16),
            shape((lines, n_tok), BF16),
            shape((rows, units), BF16),
            shape((rows, units), BF16),
            shape((rows, units), BF16),
            shape((rows, width), BF16),
            shape((rows, width), BF16),
        ),
        in_specs=[vmem] * 4 + [hbm] * 3,
        out_specs=(vmem,) * 7,
        scratch_shapes=[
            pltpu.VMEM((width, units), BF16),
            pltpu.VMEM((width, units), BF16),
            pltpu.VMEM((width, units), BF16),
            pltpu.VMEM((lines, fold_width), BF16),
            pltpu.VMEM((lines, fold_width), BF16),
            pltpu.VMEM((2 * lines, fold_width), BF16),
            pltpu.VMEM((2 * lines, fold_width), BF16),
            pltpu.VMEM((lines, fold_width), F32),
            pltpu.VMEM((rows, units), F32),
            pltpu.VMEM((rows, units), F32),
            pltpu.VMEM((rows, width), F32),
            pltpu.VMEM((rows // 2, width), BF16),
            pltpu.VMEM((rows // 2, width), BF16),
            pltpu.VMEM((lines, fold_width), BF16),
            sem((3, units // chunk)),
            sem((experts,)), sem((experts,)), sem((experts,)), sem((experts,)),
            sem((experts,)), sem((experts,)), sem((experts,)), sem((experts,)),
            sem((2,)), sem((experts,)), sem((experts,)),
        ],
        compiler_params=pltpu.CompilerParams(
            collective_id=0, has_side_effects=True, vmem_limit_bytes=56 * 1024 * 1024
        ),
        name="exchange",
    )(
        tokens.T, cotangent.T, expert_ids.T, route_weight.T,
        gate_weight.T, up_weight.T, down_weight.T,
    )

    step = fold_width // 2 if fold_width % 256 == 0 else fold_width
    per_fold = fold_width // step
    part = pl.BlockSpec((rows, step), lambda i: (0, i))
    whole = pl.BlockSpec((rows, units), lambda i: (0, 0))
    result = pl.BlockSpec((step, units), lambda i: (i, 0))
    grads = pl.pallas_call(
        functools.partial(weight_kernel, per_fold),
        out_shape=(shape((width, n_tok), BF16),) + (shape((width, units), BF16),) * 3,
        grid=(pl.cdiv(width, step),),
        in_specs=[
            whole, whole, whole, part, part,
            pl.BlockSpec((lines, step), lambda i: (0, i % per_fold)),
            pl.BlockSpec((lines, n_tok), lambda i: (0, 0)),
        ],
        out_specs=(pl.BlockSpec((step, n_tok), lambda i: (i, 0)),) + (result,) * 3,
        compiler_params=pltpu.CompilerParams(vmem_limit_bytes=56 * 1024 * 1024),
        cost_estimate=pl.CostEstimate(
            flops=6 * rows * units * width, bytes_accessed=6 * units * width, transcendentals=0
        ),
        name="weight_grads",
    )(d_gate, d_up, act, x, c, ret, place)
    return tuple(g.T for g in grads)


def expert_backward(rows_x, rows_c, w_gate, w_up, w_down):
    contract_last = (((1,), (1,)), ((), ()))
    gate_pre = lax.dot_general(rows_x, w_gate, contract_last, preferred_element_type=jnp.float32)
    up_pre = lax.dot_general(rows_x, w_up, contract_last, preferred_element_type=jnp.float32)
    d_act = lax.dot_general(rows_c, w_down, contract_last, preferred_element_type=jnp.float32)
    sigmoid_gate = jax.nn.sigmoid(1.702 * gate_pre)
    gated = gate_pre * sigmoid_gate
    activation = ((up_pre + 1.0) * gated).astype(jnp.bfloat16)
    d_up = (d_act * gated).astype(jnp.bfloat16)
    d_gate = (
        d_act
        * (up_pre + 1.0)
        * (sigmoid_gate + 1.702 * gate_pre * sigmoid_gate * (1.0 - sigmoid_gate))
    ).astype(jnp.bfloat16)
    partial_value = jnp.dot(d_gate, w_gate, preferred_element_type=jnp.float32) + jnp.dot(
        d_up, w_up, preferred_element_type=jnp.float32
    )
    return (activation, d_gate, d_up, partial_value)


def weight_terms(rows_x, rows_c, activation, d_gate, d_up):
    contract_first = (((0,), (0,)), ((), ()))
    term_gate = lax.dot_general(
        d_gate, rows_x, contract_first, preferred_element_type=jnp.float32
    ).astype(jnp.bfloat16)
    term_up = lax.dot_general(
        d_up, rows_x, contract_first, preferred_element_type=jnp.float32
    ).astype(jnp.bfloat16)
    term_down = lax.dot_general(
        activation, rows_c, contract_first, preferred_element_type=jnp.float32
    ).astype(jnp.bfloat16)
    return lax.optimization_barrier((term_gate, term_up, term_down))


def body(tokens, cotangent, expert_ids, route_weight, gate_weight, up_weight, down_weight):
    devices = lax.axis_size("expert")
    group_size = devices // E_WIN
    model_width = tokens.shape[1]
    window_ids = jnp.arange(E_WIN, dtype=jnp.int32)
    matches = expert_ids[:, :, None] == window_ids[None, None, :]
    member = jnp.any(matches, axis=1)
    weight_of = jnp.sum(jnp.where(matches, route_weight[:, :, None], 0.0), axis=1)
    position = jnp.cumsum(member.astype(jnp.int32), axis=0) - 1
    slot_ids = jnp.arange(CAP, dtype=jnp.int32)
    placement = jnp.logical_and(
        member.T[:, None, :], position.T[:, None, :] == slot_ids[None, :, None]
    )
    place_half = placement.astype(jnp.bfloat16)
    place_full = placement.astype(jnp.float32)
    picked_x = jnp.einsum(
        "kct,td->kcd", place_half, tokens, preferred_element_type=jnp.float32
    ).astype(jnp.bfloat16)
    picked_dy = jnp.einsum("kct,td->kcd", place_half, cotangent, preferred_element_type=jnp.float32)
    slot_weight = jnp.einsum("kct,tk->kc", place_full, weight_of, precision=lax.Precision.HIGHEST)
    picked_c = (slot_weight[:, :, None] * picked_dy).astype(jnp.bfloat16)
    send_x = jnp.repeat(picked_x, group_size, axis=0)
    send_c = jnp.repeat(picked_c, group_size, axis=0)
    recv_x, recv_c = (
        lax.all_to_all(send_x, "expert", split_axis=0, concat_axis=0, tiled=True),
        lax.all_to_all(send_c, "expert", split_axis=0, concat_axis=0, tiled=True),
    )
    rows_x = recv_x.reshape(devices * CAP, model_width)
    rows_c = recv_c.reshape(devices * CAP, model_width)
    full_gate, full_up, full_down = (
        lax.all_gather(gate_weight, "dp", axis=0, tiled=True),
        lax.all_gather(up_weight, "dp", axis=0, tiled=True),
        lax.all_gather(down_weight, "dp", axis=0, tiled=True),
    )
    activation, d_gate, d_up, partial_value = expert_backward(
        rows_x, rows_c, full_gate, full_up, full_down
    )
    part_rows = partial_value.astype(jnp.bfloat16)
    term_gate, term_up, term_down = weight_terms(rows_x, rows_c, activation, d_gate, d_up)
    summed = (
        lax.psum_scatter(
            term_gate.astype(jnp.float32).astype(jnp.bfloat16),
            "dp",
            scatter_dimension=0,
            tiled=True,
        ).astype(jnp.float32),
        lax.psum_scatter(
            term_up.astype(jnp.float32).astype(jnp.bfloat16), "dp", scatter_dimension=0, tiled=True
        ).astype(jnp.float32),
        lax.psum_scatter(
            term_down.astype(jnp.float32).astype(jnp.bfloat16),
            "dp",
            scatter_dimension=0,
            tiled=True,
        ).astype(jnp.float32),
    )
    grad_gate = summed[0].astype(jnp.bfloat16)
    grad_up = summed[1].astype(jnp.bfloat16)
    grad_down = summed[2].astype(jnp.bfloat16)
    returned = lax.all_to_all(
        part_rows.reshape(devices, CAP, model_width),
        "expert",
        split_axis=0,
        concat_axis=0,
        tiled=True,
    )
    combined = jnp.sum(
        returned.astype(jnp.float32).reshape(E_WIN, group_size, CAP, model_width), axis=1
    )
    grad_tokens = jnp.einsum(
        "kct,kcd->td", place_full, combined, precision=lax.Precision.HIGHEST
    ).astype(jnp.bfloat16)
    return (grad_tokens, grad_gate, grad_up, grad_down)


def solution(mesh):
    sizes = mesh.shape
    return jax.shard_map(
        kernel_body if sizes["expert"] == E_WIN and sizes["dp"] == 2 else body,
        mesh=mesh,
        in_specs=(
            P(("groups", "expert", "dp"), None),
            P(("groups", "expert", "dp"), None),
            P(("groups", "expert", "dp"), None),
            P(("groups", "expert", "dp"), None),
            P(("expert", "dp"), None),
            P(("expert", "dp"), None),
            P(("expert", "dp"), None),
        ),
        out_specs=(
            P(("groups", "expert", "dp"), None),
            P(("groups", "expert", "dp"), None),
            P(("groups", "expert", "dp"), None),
            P(("groups", "expert", "dp"), None),
        ),
        check_vma=False,
    )
```
